512 devices in a mesh: row: 32 (over x, y, core), col: 16 (over z).
Axes of the slice: x: 4, y: 4, z: 16, core: 2. Of those that a mesh axis runs over, the one named last changes fastest.
Arguments:
- blocks: float32 [32, 192, 256, 256], P('row', 'col'), may hold values from -0.078125 to 0.078125
- block_rows: int32 [32, 192], P('row', 'col'), may hold values from 0 to 3, as said below
- block_cols: int32 [32, 192], P('row', 'col'), may hold values from 0 to 7
- live_count: int32 [32, 16], P('row', 'col'), may hold values from 1 to 12
- primal_now: float32 [16, 2048, 128], P('col', 'row'), may hold values from -3 to 3
- primal_prev: float32 [16, 2048, 128], P('col', 'row'), may hold values from -3 to 3
- dual_now: float32 [32, 1024, 128], P('row', 'col'), may hold values from 0 to 1
- row_bound: float32 [32, 1024, 128], P('row', 'col'), may hold values from -6 to 6
- objective: float32 [16, 2048, 128], P('col', 'row'), may hold values from -6 to 6
- lower_bound: float32 [16, 2048, 128], P('col', 'row'), may hold values from -1 to -0.2
- upper_bound: float32 [16, 2048, 128], P('col', 'row'), may hold values from 0.2 to 1
Outputs:
- primal_out: float32 [16, 2048, 128], P('col', 'row')
- dual_out: float32 [32, 1024, 128], P('row', 'col')
The draws below stay inside these ranges and needn't reach their ends.
Inputs may be any that keep to these rules, and one draw needn't show every extreme that they name: On each device the 12 pairs (block_rows, block_cols) are distinct.
All inputs are finite; a program needn't handle non-finite values.
Results may differ from the reference program's by a relative error of at most 0.0001.
Values sent between devices are 32-bit elements; how exact they have to be, the bound alone decides.
A program may use at most 64 MiB of HBM per device.

```python
import jax
import jax.numpy as jnp
from jax import lax

BS = 256
RB_DEV = 4
CB_DEV = 8
SLOTS = 12
BATCH = 128
ITERS = 2
N_ROW = 32
N_COL = 16


def slot_places(key):
    device_keys = jax.random.split(key, N_ROW * N_COL)
    orders = jax.vmap(lambda one_key: jax.random.permutation(one_key, RB_DEV * CB_DEV))(device_keys)
    return orders[:, :SLOTS].reshape(N_ROW, N_COL * SLOTS).astype(jnp.int32)


def draw_block_rows(key, part):
    places = slot_places(key)
    return (places // CB_DEV).astype(jnp.int32)


def draw_block_cols(key, part):
    places = slot_places(key)
    return (places % CB_DEV).astype(jnp.int32)


def draw_live_count(key, part):
    key = jax.random.fold_in(key, 3)
    first, second, third = jax.random.split(key, 3)
    devices = N_ROW * N_COL
    counts = jax.random.randint(first, (devices,), 1, SLOTS + 1).astype(jnp.int32)
    fullest = jax.random.randint(second, (), 0, devices).astype(jnp.int32)
    offset = jax.random.randint(third, (), 0, devices - 1).astype(jnp.int32)
    counts = counts.at[fullest].set(SLOTS)
    counts = counts.at[(fullest + 1 + offset) % devices].set(1)
    return counts.reshape(N_ROW, N_COL).astype(jnp.int32)


def block_levels(stream_key, shape, cuts, least, top_value):
    def one(axis_at, parts):
        draws = jax.random.uniform(jax.random.fold_in(jax.random.fold_in(stream_key, 6), axis_at), (parts,), jnp.float32, least / len(cuts), top_value / len(cuts))
        return jnp.repeat(jnp.exp(draws), shape[axis_at] // parts).reshape((-1,) + (1,) * (len(shape) - axis_at - 1))

    factor_of = one(*cuts[0])
    for cut in cuts[1:]:
        factor_of = factor_of * one(*cut)
    return factor_of


def scatter_about(rng, extent, deviation, reach, pieces=(), held_as=jnp.bfloat16):
    factor_of = block_levels(rng, extent, pieces, -0.22, 0.18) if pieces else 1.0
    values = jax.random.normal(rng, extent, jnp.float32) * deviation * factor_of
    return jnp.minimum(jnp.maximum(values, -reach), reach).astype(held_as)


def setup_inputs(seed: int = 0) -> dict:
    arg_keys = jax.random.split(jax.random.key(seed), 12)
    blocks = scatter_about(arg_keys[0], (N_ROW, N_COL * SLOTS, BS, BS), (BS * SLOTS * N_COL // (2 * RB_DEV)) ** -0.5, 0.078125, ((0, 32), (1, 16)), jnp.float32)
    block_rows = draw_block_rows(jax.random.fold_in(arg_keys[11], 71), 0)
    block_cols = draw_block_cols(jax.random.fold_in(arg_keys[11], 71), 0)
    live_count = draw_live_count(jax.random.fold_in(arg_keys[11], 71), 0)
    primal_now = scatter_about(arg_keys[4], (N_COL, CB_DEV * BS, BATCH), 0.5, 3.0, ((0, 16), (1, 32)), jnp.float32)
    primal_prev = scatter_about(arg_keys[5], (N_COL, CB_DEV * BS, BATCH), 0.5, 3.0, ((0, 16), (1, 32)), jnp.float32)
    dual_now = jnp.clip(1.0 * jax.random.uniform(arg_keys[6], (N_ROW, RB_DEV * BS, BATCH), jnp.float32) ** block_levels(arg_keys[6], (N_ROW, RB_DEV * BS, BATCH), ((0, 32), (1, 16)), -0.2, 0.2), 0.0, 1.0)
    row_bound = scatter_about(arg_keys[7], (N_ROW, RB_DEV * BS, BATCH), 1.0, 6.0, ((0, 32), (1, 16)), jnp.float32)
    objective = scatter_about(arg_keys[8], (N_COL, CB_DEV * BS, BATCH), 1.0, 6.0, ((0, 16), (1, 32)), jnp.float32)
    lower_bound = jnp.clip(-1.0 + 0.8 * jax.random.uniform(arg_keys[9], (N_COL, CB_DEV * BS, BATCH), jnp.float32) ** block_levels(arg_keys[9], (N_COL, CB_DEV * BS, BATCH), ((0, 16), (1, 32)), -0.2, 0.2), -1.0, -0.2)
    upper_bound = jnp.clip(0.2 + 0.8 * jax.random.uniform(arg_keys[10], (N_COL, CB_DEV * BS, BATCH), jnp.float32) ** block_levels(arg_keys[10], (N_COL, CB_DEV * BS, BATCH), ((0, 16), (1, 32)), -0.2, 0.2), 0.2, 1.0)
    return dict(blocks=blocks, block_rows=block_rows, block_cols=block_cols, live_count=live_count, primal_now=primal_now, primal_prev=primal_prev, dual_now=dual_now, row_bound=row_bound, objective=objective, lower_bound=lower_bound, upper_bound=upper_bound)


dual_step = 0.3
primal_step = 0.3


def reference(blocks, block_rows, block_cols, live_count, primal_now, primal_prev, dual_now, row_bound, objective, lower_bound, upper_bound):
    highest = lax.Precision.HIGHEST
    tiles = blocks.reshape(N_ROW, N_COL, SLOTS, BS, BS)
    in_use = (jnp.arange(SLOTS, dtype=jnp.int32)[None, None, :] < live_count[:, :, None]).astype(jnp.float32)
    row_pick = jax.nn.one_hot(block_rows.reshape(N_ROW, N_COL, SLOTS), RB_DEV, dtype=jnp.float32)
    col_pick = jax.nn.one_hot(block_cols.reshape(N_ROW, N_COL, SLOTS), CB_DEV, dtype=jnp.float32)
    row_live = row_pick * in_use[..., None]
    col_live = col_pick * in_use[..., None]
    scenarios = primal_now.shape[2]

    def forward(extrapolated):
        spread = extrapolated.reshape(N_COL, CB_DEV, BS, scenarios)

        def one_row(items):
            tile_row, cols_here, rows_here = items
            picked = jnp.einsum('nsc,ncjb->nsjb', cols_here, spread, precision=highest)
            product = jnp.einsum('nsij,nsjb->nsib', tile_row, picked, precision=highest)
            return jnp.einsum('nsr,nsib->rib', rows_here, product, precision=highest).reshape(RB_DEV * BS, scenarios)

        return lax.map(one_row, (tiles, col_live, row_pick))

    def backward(dual_vec):
        spread = dual_vec.reshape(N_ROW, RB_DEV, BS, scenarios)

        def one_row(carry, items):
            tile_row, cols_here, rows_here, dual_row = items
            picked = jnp.einsum('nsr,rib->nsib', rows_here, dual_row, precision=highest)
            product = jnp.einsum('nsij,nsib->nsjb', tile_row, picked, precision=highest)
            return carry + jnp.einsum('nsc,nsjb->ncjb', cols_here, product, precision=highest), None

        start = jnp.zeros((N_COL, CB_DEV, BS, scenarios), jnp.float32)
        summed, _ = lax.scan(one_row, start, (tiles, col_pick, row_live, spread))
        return summed.reshape(N_COL, CB_DEV * BS, scenarios)

    current = primal_now
    previous = primal_prev
    dual_vec = dual_now
    for step in range(ITERS):
        extrapolated = 2.0 * current - previous
        image = forward(extrapolated)
        dual_vec = jnp.maximum(dual_vec + dual_step * (row_bound - image), 0.0)
        adjoint = backward(dual_vec)
        previous = current
        current = jnp.minimum(jnp.maximum(current - primal_step * (objective - adjoint), lower_bound), upper_bound)
    return current, dual_vec
```

```python
import functools

import jax
import jax.numpy as jnp
from jax import lax
from jax.experimental import pallas as pl
from jax.experimental.pallas import tpu as pltpu
from jax.sharding import PartitionSpec as P

MESH = pl.DeviceIdType.MESH
F32 = jnp.float32
BF16 = jnp.bfloat16

NX, NY, NZ = 4, 4, 16
RB_DEV = 4
CB_DEV = 8
SLOTS = 12
BS = 256
ITERS = 2
BATCH = 128
CHUNK = 64
HALF = CHUNK // 2
PARTS = BS // CHUNK

dual_step = 0.3
primal_step = 0.3

SIDES = (1, -1)
XY_PARTNERS = sorted(
    [(dx, dy) for dx in range(NX) for dy in range(NY) if (dx, dy) != (0, 0)],
    key=lambda d: -(min(d[0], NX - d[0]) + min(d[1], NY - d[1])),
)
FROM7, FROM6, FROM4, FROM8, FROM3, SUM5, SUM2, NEXT = range(8)
FIRST_HOPS = ((FROM8, 8, 3), (FROM7, 7, 2), (FROM6, 6, 1), (FROM4, 4, -1), (FROM3, 3, 1), (NEXT, 1, 1))


def split(value):
    high = value.astype(BF16)
    low = (value - high.astype(F32)).astype(BF16)
    return high, low


def kernel(
    rows_ref, cols_ref, live_ref,
    blocks_hbm, now_ref, prev_ref, dual_ref, bound_ref, cost_ref, lower_ref, upper_ref,
    primal_out, dual_out,
    place,
    blk, a_hi, a_lo, at_hi, at_lo,
    xg, xs, prod, ys, rz, dg, ds, zs, zc, rx, cur,
    blk_sem,
    xg_send, xg_recv, xc_send, xc_recv,
    rz_send, rz_recv, dg_send, dg_recv,
    zc_send, zc_recv, rx_send, rx_recv,
):
    row = lax.axis_index("row")
    z = lax.axis_index("col")
    x = row // (2 * NY)
    y = (row // 2) % NY
    core = row % 2
    other = 1 - core

    def wrap(value, size):
        return lax.rem(value + size, size)

    def plane(dx, dy):
        return (wrap(x + dx, NX) * (2 * NY) + wrap(y + dy, NY) * 2 + core, z)

    def along(dz):
        return (row, wrap(z + dz, NZ))

    sibling = (row + 1 - 2 * core, z)

    load = pltpu.make_async_copy(blocks_hbm, blk, blk_sem)
    load.start()

    barrier = pltpu.get_barrier_semaphore()
    greeted = [sibling] + [plane(dx, dy) for dx, dy in XY_PARTNERS]
    greeted += [along(sg * d) for d in (1, 2, 3, 5) for sg in SIDES]
    for device in greeted:
        pl.semaphore_signal(barrier, inc=1, device_id=device, device_id_type=MESH)
    pl.semaphore_wait(barrier, len(greeted))

    sends = []

    def send(src, dst, send_sem, recv_sem, device):
        copy = pltpu.make_async_remote_copy(
            src_ref=src, dst_ref=dst, send_sem=send_sem, recv_sem=recv_sem,
            device_id=device, device_id_type=MESH,
        )
        copy.start()
        sends.append(copy)
        return copy

    def gather_plane_start(it, value):
        own = xg.at[it, core, x, y]
        own[...] = value
        copies = {}
        for dx, dy in XY_PARTNERS:
            k = dx * NY + dy
            copies[dx, dy] = send(own, own, xg_send.at[it, k], xg_recv.at[it, k], plane(dx, dy))
        return copies

    def split_group(it, c, gx):
        for gy in range(NY):
            high, low = split(xg[it, c, gx, gy])
            at = gx * (2 * NY) + gy * 2 + c
            xs[at, :, :BATCH] = high
            xs[at, :, BATCH:] = low

    def gather_plane_finish(it, copies):
        forwards = []
        for dx in (0, 1, 3, 2):
            gx = wrap(x - dx, NX)
            for dy in range(NY):
                if (dx, dy) != (0, 0):
                    copies[dx, dy].wait_recv()
            group = xg.at[it, core, gx]
            forwards.append(send(group, group, xc_send.at[it, dx], xc_recv.at[it, dx], sibling))
            split_group(it, core, gx)
        for dx, copy in zip((0, 1, 3, 2), forwards):
            copy.wait_recv()
            split_group(it, other, wrap(x - dx, NX))

    def products(hi, lo, table, vec):
        for s in range(SLOTS):
            at = table[s]
            rhs = vec[pl.ds(at * PARTS, PARTS)].reshape(BS, 2 * BATCH)
            main = jnp.dot(hi[s], rhs, preferred_element_type=F32)
            rest = jnp.dot(lo[s], rhs[:, :BATCH], preferred_element_type=F32)
            prod[s] = (main[:, :BATCH] + main[:, BATCH:] + rest).reshape(PARTS, CHUNK, BATCH)

    def image_chunk(zd):
        r, part = zd // PARTS, zd % PARTS
        total = prod[place[r * CB_DEV], part]
        for c in range(1, CB_DEV):
            total += prod[place[r * CB_DEV + c], part]
        return total

    def adjoint_chunk(at):
        cb, part = at // PARTS, at % PARTS
        total = prod[place[cb], part]
        for r in range(1, RB_DEV):
            total += prod[place[r * CB_DEV + cb], part]
        return total

    def half(sg):
        return pl.ds(0 if sg == 1 else HALF, HALF)

    def reduce_ring(it):
        hops = {}
        for slot, far, via in FIRST_HOPS:
            for sg in SIDES:
                zd = wrap(z + sg * far, NZ)
                if not (slot == FROM8 and sg == -1):
                    ys[it, zd] = image_chunk(zd)
                src, dst = ys.at[it, zd], rz.at[it, (1 - sg) // 2, slot]
                if slot == FROM8:
                    src, dst = src.at[half(sg)], dst.at[half(sg)]
                sem = (it, (1 - sg) // 2, slot)
                hops[slot, sg] = send(src, dst, rz_send.at[sem], rz_recv.at[sem], along(sg * via))
        for far in (2, 5):
            for sg in SIDES:
                zd = wrap(z + sg * far, NZ)
                ys[it, zd] = image_chunk(zd)
        mine = image_chunk(z)
        for slot, far, parts in ((SUM5, 5, (FROM4, FROM6, FROM7, FROM8)), (SUM2, 2, (FROM3,))):
            for sg in SIDES:
                side = (1 - sg) // 2
                zd = wrap(z + sg * far, NZ)
                for part in parts:
                    hops[part, sg].wait_recv()
                    if part == FROM8:
                        ys[it, zd, half(sg)] += rz[it, side, part, half(sg)]
                    else:
                        ys[it, zd] += rz[it, side, part]
                sem = (it, side, slot)
                hops[slot, sg] = send(
                    ys.at[it, zd], rz.at[it, side, slot], rz_send.at[sem], rz_recv.at[sem], along(sg * far)
                )
        for slot in (NEXT, SUM2, SUM5):
            for sg in SIDES:
                hops[slot, sg].wait_recv()
                mine += rz[it, (1 - sg) // 2, slot]
        return mine

    def gather_ring(it, value):
        copies = {}

        def pass_on(far, via):
            at = wrap(z + via - far, NZ)
            ref = dg.at[it, at]
            sem = (it, far % NZ)
            if abs(far) == 8:
                sg = 1 if far == 8 else -1
                ref = ref.at[half(sg)]
                sem = (it, 8 if sg == 1 else 0)
            copies[far] = send(ref, ref, dg_send.at[sem], dg_recv.at[sem], along(via))

        def split_chunk(far):
            at = wrap(z - far, NZ)
            high, low = split(dg[it, at])
            ds[at, :, :BATCH] = high
            ds[at, :, BATCH:] = low

        dg[it, z] = value
        for far in (5, 2, 1):
            for sg in SIDES:
                pass_on(sg * far, sg * far)
        split_chunk(0)
        for sg in SIDES:
            copies[sg].wait_recv()
            split_chunk(sg)
        for sg in SIDES:
            copies[2 * sg].wait_recv()
            pass_on(3 * sg, sg)
            split_chunk(2 * sg)
        for sg in SIDES:
            copies[5 * sg].wait_recv()
            pass_on(8 * sg, 3 * sg)
            pass_on(7 * sg, 2 * sg)
            pass_on(6 * sg, sg)
            pass_on(4 * sg, -sg)
        for sg in SIDES:
            split_chunk(5 * sg)
        for far in (3, 4, 6, 7):
            for sg in SIDES:
                copies[sg * far].wait_recv()
                split_chunk(sg * far)
        copies[8].wait_recv()
        copies[-8].wait_recv()
        split_chunk(8)

    def reduce_plane(it):
        order = (2, 1, 3, 0)
        swaps = []
        for dx in order:
            gx = wrap(x + dx, NX)
            for gy in range(NY):
                zs[it, other, gx, gy] = adjoint_chunk(gx * (2 * NY) + gy * 2 + other)
            swaps.append(
                send(zs.at[it, other, gx], zc.at[it, gx], zc_send.at[it, dx], zc_recv.at[it, dx], sibling)
            )
        for dx in order:
            gx = wrap(x + dx, NX)
            for gy in range(NY):
                zs[it, core, gx, gy] = adjoint_chunk(gx * (2 * NY) + gy * 2 + core)
        copies = {}
        for dx, swap in zip(order, swaps):
            gx = wrap(x + dx, NX)
            swap.wait_recv()
            for dy in (2, 1, 3, 0):
                gy = wrap(y + dy, NY)
                zs[it, core, gx, gy] += zc[it, gx, gy]
                if (dx, dy) != (0, 0):
                    k = dx * NY + dy
                    copies[dx, dy] = send(
                        zs.at[it, core, gx, gy], rx.at[it, k], rx_send.at[it, k], rx_recv.at[it, k], plane(dx, dy)
                    )
        total = zs[it, core, x, y]
        for dx, dy in reversed(XY_PARTNERS):
            copies[dx, dy].wait_recv()
            total += rx[it, dx * NY + dy]
        return total

    gathers = gather_plane_start(0, 2.0 * now_ref[...] - prev_ref[...])
    cur[...] = now_ref[...]

    prod[SLOTS] = jnp.zeros((PARTS, CHUNK, BATCH), F32)
    live = live_ref[0, 0]
    keys = [
        jnp.where(s < live, rows_ref[0, s] * CB_DEV + cols_ref[0, s], -1) for s in range(SLOTS)
    ]
    for b in range(RB_DEV * CB_DEV):
        found = jnp.int32(SLOTS)
        for s in range(SLOTS):
            found = jnp.where(keys[s] == b, s, found)
        place[b] = found
    load.wait()

    def prepare(s, carry):
        value = blk[s]
        high, low = split(value)
        a_hi[s] = high
        a_lo[s] = low
        high, low = split(value.T)
        at_hi[s] = high
        at_lo[s] = low
        return carry

    lax.fori_loop(0, SLOTS, prepare, 0)

    dual = dual_ref[...]
    for it in range(ITERS):
        gather_plane_finish(it, gathers)
        products(a_hi, a_lo, [cols_ref[0, s] for s in range(SLOTS)], xs)
        image = reduce_ring(it)
        dual = jnp.maximum(dual + dual_step * (bound_ref[...] - image), 0.0)
        gather_ring(it, dual)
        products(at_hi, at_lo, [rows_ref[0, s] for s in range(SLOTS)], ds)
        adjoint = reduce_plane(it)
        before = cur[...]
        after = jnp.minimum(
            jnp.maximum(before - primal_step * (cost_ref[...] - adjoint), lower_ref[...]), upper_ref[...]
        )
        if it + 1 < ITERS:
            gathers = gather_plane_start(it + 1, 2.0 * after - before)
            cur[...] = after
        else:
            primal_out[...] = after
            dual_out[...] = dual
    for copy in sends:
        copy.wait_send()


def on_device(
    blocks, block_rows, block_cols, live_count, primal_now, primal_prev, dual_now, row_bound,
    objective, lower_bound, upper_bound,
):
    vmem = pl.BlockSpec(memory_space=pltpu.VMEM)
    smem = pl.BlockSpec(memory_space=pltpu.SMEM)
    dma = pltpu.SemaphoreType.DMA
    vec = jax.ShapeDtypeStruct((CHUNK, BATCH), F32)
    primal, dual = pl.pallas_call(
        kernel,
        out_shape=(vec, vec),
        in_specs=[smem] * 3 + [pl.BlockSpec(memory_space=pl.ANY)] + [vmem] * 7,
        out_specs=(vmem, vmem),
        scratch_shapes=[
            pltpu.SMEM((RB_DEV * CB_DEV,), jnp.int32),
            pltpu.VMEM((SLOTS, BS, BS), F32),
            pltpu.VMEM((SLOTS, BS, BS), BF16),
            pltpu.VMEM((SLOTS, BS, BS), BF16),
            pltpu.VMEM((SLOTS, BS, BS), BF16),
            pltpu.VMEM((SLOTS, BS, BS), BF16),
            pltpu.VMEM((ITERS, 2, NX, NY, CHUNK, BATCH), F32),
            pltpu.VMEM((2 * NX * NY, CHUNK, 2 * BATCH), BF16),
            pltpu.VMEM((SLOTS + 1, PARTS, CHUNK, BATCH), F32),
            pltpu.VMEM((ITERS, NZ, CHUNK, BATCH), F32),
            pltpu.VMEM((ITERS, 2, 8, CHUNK, BATCH), F32),
            pltpu.VMEM((ITERS, NZ, CHUNK, BATCH), F32),
            pltpu.VMEM((NZ, CHUNK, 2 * BATCH), BF16),
            pltpu.VMEM((ITERS, 2, NX, NY, CHUNK, BATCH), F32),
            pltpu.VMEM((ITERS, NX, NY, CHUNK, BATCH), F32),
            pltpu.VMEM((ITERS, NX * NY, CHUNK, BATCH), F32),
            pltpu.VMEM((CHUNK, BATCH), F32),
            dma,
            dma((ITERS, NX * NY)), dma((ITERS, NX * NY)),
            dma((ITERS, NX)), dma((ITERS, NX)),
            dma((ITERS, 2, 8)), dma((ITERS, 2, 8)),
            dma((ITERS, NZ)), dma((ITERS, NZ)),
            dma((ITERS, NX)), dma((ITERS, NX)),
            dma((ITERS, NX * NY)), dma((ITERS, NX * NY)),
        ],
        compiler_params=pltpu.CompilerParams(
            collective_id=0, has_side_effects=True, vmem_limit_bytes=48 * 1024 * 1024
        ),
        name="pdhg",
    )(
        block_rows, block_cols, live_count,
        blocks[0], primal_now[0], primal_prev[0], dual_now[0], row_bound[0],
        objective[0], lower_bound[0], upper_bound[0],
    )
    return (primal[None], dual[None])


def solution(mesh):
    in_specs = (
        P("row", "col", None, None),
        P("row", "col"),
        P("row", "col"),
        P("row", "col"),
        P("col", "row", None),
        P("col", "row", None),
        P("row", "col", None),
        P("row", "col", None),
        P("col", "row", None),
        P("col", "row", None),
        P("col", "row", None),
    )
    out_specs = (P("col", "row", None), P("row", "col", None))
    return jax.shard_map(
        on_device, mesh=mesh, in_specs=in_specs, out_specs=out_specs, check_vma=False
    )
```

```python
import functools

import jax
import jax.numpy as jnp
from jax import lax
from jax.experimental import pallas as pl
from jax.experimental.pallas import tpu as pltpu
from jax.sharding import PartitionSpec as P

MESH = pl.DeviceIdType.MESH
F32 = jnp.float32
BF16 = jnp.bfloat16

NX, NY, NZ = 4, 4, 16
RB_DEV = 4
CB_DEV = 8
SLOTS = 12
BS = 256
ITERS = 2
BATCH = 128
CHUNK = 64
HALF = CHUNK // 2
PARTS = BS // CHUNK

dual_step = 0.3
primal_step = 0.3

SIDES = (1, -1)
XY_PARTNERS = sorted(
    [(dx, dy) for dx in range(NX) for dy in range(NY) if (dx, dy) != (0, 0)],
    key=lambda d: -(min(d[0], NX - d[0]) + min(d[1], NY - d[1])),
)
FROM3, FROM4, FROM6, FROM7, FROM8, NEXT, SUM2, SUM5 = range(8)
FIRST_HOPS = ((FROM8, 8, 3), (FROM7, 7, 2), (FROM6, 6, 1), (FROM4, 4, -1), (FROM3, 3, 1), (NEXT, 1, 1))
SLOT_SUM = {FROM8: 0, FROM7: 0, FROM6: 0, FROM4: 0, FROM3: 1, NEXT: 2}
NOW, PREV, DUAL, BOUND, COST, LOWER, UPPER = range(7)


def split(value):
    high = value.astype(BF16)
    low = (value - high.astype(F32)).astype(BF16)
    return high, low


def kernel(
    rows_hbm, cols_hbm, live_hbm, blocks_hbm,
    now_hbm, prev_hbm, dual_hbm, bound_hbm, cost_hbm, lower_hbm, upper_hbm,
    primal_out, dual_out,
    rows_ref, cols_ref, live_ref, place,
    vecs, blk, a_hi, a_lo, at_hi, at_lo,
    xg, xs, prod, ys, rz, dg, ds, zs, zc, rx,
    blk_sem, list_sem, vec_sem,
    xg_send, xg_recv, xc_send, xc_recv,
    rz_send, rz_recv, dg_send, dg_recv,
    zc_send, zc_recv, rx_send, rx_recv,
):
    row = lax.axis_index("row")
    z = lax.axis_index("col")
    x = row // (2 * NY)
    y = (row // 2) % NY
    core = row % 2
    other = 1 - core

    def wrap(value, size):
        return lax.rem(value + size, size)

    def plane(dx, dy):
        return (wrap(x + dx, NX) * (2 * NY) + wrap(y + dy, NY) * 2 + core, z)

    def along(dz):
        return (row, wrap(z + dz, NZ))

    sibling = (row + 1 - 2 * core, z)

    barrier = pltpu.get_barrier_semaphore()
    greeted = [sibling] + [plane(dx, dy) for dx, dy in XY_PARTNERS]
    greeted += [along(sg * d) for d in (1, 2, 3, 5) for sg in SIDES]
    for device in greeted:
        pl.semaphore_signal(barrier, inc=1, device_id=device, device_id_type=MESH)

    vec_refs = (now_hbm, prev_hbm, dual_hbm, bound_hbm, cost_hbm, lower_hbm, upper_hbm)
    vec_loads = [pltpu.make_async_copy(ref, vecs.at[i], vec_sem.at[i]) for i, ref in enumerate(vec_refs)]
    list_loads = [
        pltpu.make_async_copy(src, dst, list_sem.at[i])
        for i, (src, dst) in enumerate(((rows_hbm, rows_ref), (cols_hbm, cols_ref), (live_hbm, live_ref)))
    ]
    load = pltpu.make_async_copy(blocks_hbm, blk, blk_sem)
    for copy in vec_loads[:2] + [load] + list_loads + vec_loads[2:]:
        copy.start()

    def send(src, dst, send_sem, recv_sem, device):
        copy = pltpu.make_async_remote_copy(
            src_ref=src, dst_ref=dst, send_sem=send_sem, recv_sem=recv_sem,
            device_id=device, device_id_type=MESH,
        )
        copy.start()
        return copy

    def waiter(ref, send_sem, recv_sem):
        return pltpu.make_async_remote_copy(
            src_ref=ref, dst_ref=ref, send_sem=send_sem, recv_sem=recv_sem,
            device_id=sibling, device_id_type=MESH,
        )

    def arrived(ref, recv_sem):
        waiter(ref, recv_sem, recv_sem).wait_recv()

    def half(h):
        return pl.ds(h * HALF, HALF)

    def gather_plane_start(it, h, value):
        own = xg.at[it, h, core, x, y]
        own[...] = value
        for dx, dy in XY_PARTNERS:
            send(own, own, xg_send.at[it, h], xg_recv.at[it, h, dx], plane(dx, dy))

    def split_group(it, h, c, gx):
        for gy in range(NY):
            high, low = split(xg[it, h, c, gx, gy])
            at = gx * (2 * NY) + gy * 2 + c
            xs[at, half(h), :BATCH] = high
            xs[at, half(h), BATCH:] = low

    def gather_plane_pass(it, h):
        for dx in (0, 1, 3, 2):
            gx = wrap(x - dx, NX)
            group = xg.at[it, h, core, gx]
            arrived(group if dx else group.at[pl.ds(0, NY - 1)], xg_recv.at[it, h, dx])
            send(group, group, xc_send.at[it, h], xc_recv.at[it, h, dx], sibling)
            split_group(it, h, core, gx)

    def gather_plane_last(it, h):
        for dx in (0, 1, 3, 2):
            gx = wrap(x - dx, NX)
            arrived(xg.at[it, h, other, gx], xc_recv.at[it, h, dx])
            split_group(it, h, other, gx)

    def products(hi, lo, table, vec):
        for s in range(SLOTS):
            at = table[s]
            rhs = vec[pl.ds(at * PARTS, PARTS)].reshape(BS, 2 * BATCH)
            main = jnp.dot(hi[s], rhs, preferred_element_type=F32)
            rest = jnp.dot(lo[s], rhs[:, :BATCH], preferred_element_type=F32)
            prod[s] = (main[:, :BATCH] + main[:, BATCH:] + rest).reshape(PARTS, 2, HALF, BATCH)

    def image_chunk(h, zd):
        r, part = zd // PARTS, zd % PARTS
        total = prod[place[r * CB_DEV], part, h]
        for c in range(1, CB_DEV):
            total += prod[place[r * CB_DEV + c], part, h]
        return total

    def adjoint_chunk(h, at):
        cb, part = at // PARTS, at % PARTS
        total = prod[place[cb], part, h]
        for r in range(1, RB_DEV):
            total += prod[place[r * CB_DEV + cb], part, h]
        return total

    def side(sg):
        return (1 - sg) // 2

    def has(h, sg, slot):
        return slot != FROM8 or side(sg) == h

    def ring_send(it, h):
        for slot, far, via in FIRST_HOPS:
            for sg in SIDES:
                if has(h, sg, slot):
                    zd = wrap(z + sg * far, NZ)
                    ys[it, h, zd] = image_chunk(h, zd)
                    to = SLOT_SUM[slot]
                    send(
                        ys.at[it, h, zd], rz.at[it, h, side(sg), slot],
                        rz_send.at[it, h], rz_recv.at[it, h, side(sg), to], along(sg * via),
                    )
        for far in (2, 5, 0):
            for sg in SIDES[: 2 if far else 1]:
                zd = wrap(z + sg * far, NZ)
                ys[it, h, zd] = image_chunk(h, zd)

    def ring_relay(it, h):
        for to, far, parts in ((1, 2, (FROM3,)), (0, 5, (FROM4, FROM6, FROM7, FROM8))):
            for sg in SIDES:
                zd = wrap(z + sg * far, NZ)
                parts_here = [part for part in parts if has(h, sg, part)]
                first, count = parts_here[0], len(parts_here)
                arrived(rz.at[it, h, side(sg), pl.ds(first, count)], rz_recv.at[it, h, side(sg), to])
                total = ys[it, h, zd]
                for part in parts_here:
                    total += rz[it, h, side(sg), part]
                ys[it, h, zd] = total
                slot = SUM5 if far == 5 else SUM2
                send(
                    ys.at[it, h, zd], rz.at[it, h, side(sg), slot],
                    rz_send.at[it, h], rz_recv.at[it, h, side(sg), 2], along(sg * far),
                )

    def ring_sum(it, h):
        total = ys[it, h, z]
        for sg in SIDES:
            arrived(rz.at[it, h, side(sg), pl.ds(NEXT, 3)], rz_recv.at[it, h, side(sg), 2])
            for slot in (NEXT, SUM2, SUM5):
                total += rz[it, h, side(sg), slot]
        return total

    def ring_pass(it, h, far, via):
        ref = dg.at[it, h, wrap(z + via - far, NZ)]
        sem = far % NZ if abs(far) in (1, 2, 5) else 0
        send(ref, ref, dg_send.at[it, h], dg_recv.at[it, h, sem], along(via))

    def ring_split(it, h, far):
        at = wrap(z - far, NZ)
        high, low = split(dg[it, h, at])
        ds[at, half(h), :BATCH] = high
        ds[at, half(h), BATCH:] = low

    def ring_arrived(it, h, far):
        arrived(dg.at[it, h, 0], dg_recv.at[it, h, far % NZ])

    def gather_ring_start(it, h, value):
        dg[it, h, z] = value
        for far in (5, 2, 1):
            for sg in SIDES:
                ring_pass(it, h, sg * far, sg * far)
        ring_split(it, h, 0)

    def gather_ring_relay(it, h):
        for sg in SIDES:
            ring_arrived(it, h, 2 * sg)
            ring_pass(it, h, 3 * sg, sg)
        for sg in SIDES:
            ring_arrived(it, h, 5 * sg)
            if has(h, sg, FROM8):
                ring_pass(it, h, 8 * sg, 3 * sg)
            ring_pass(it, h, 7 * sg, 2 * sg)
            ring_pass(it, h, 6 * sg, sg)
            ring_pass(it, h, 4 * sg, -sg)
        for sg in SIDES:
            ring_arrived(it, h, sg)
            for far in (1, 2, 5):
                ring_split(it, h, far * sg)

    def gather_ring_finish(it, h):
        arrived(dg.at[it, h, pl.ds(0, 9)], dg_recv.at[it, h, 0])
        for far in (3, 4, 6, 7):
            for sg in SIDES:
                ring_split(it, h, sg * far)
        ring_split(it, h, 8)

    plane_order = (2, 1, 3, 0)

    def plane_swap(it, h):
        for dx in plane_order:
            gx = wrap(x + dx, NX)
            for gy in range(NY):
                zs[it, h, other, gx, gy] = adjoint_chunk(h, gx * (2 * NY) + gy * 2 + other)
            send(
                zs.at[it, h, other, gx], zc.at[it, h, gx],
                zc_send.at[it, h], zc_recv.at[it, h, dx], sibling,
            )

    def plane_send(it, h):
        for dx in plane_order:
            gx = wrap(x + dx, NX)
            for gy in range(NY):
                zs[it, h, core, gx, gy] = adjoint_chunk(h, gx * (2 * NY) + gy * 2 + core)
        for dx in plane_order:
            gx = wrap(x + dx, NX)
            arrived(zc.at[it, h, gx], zc_recv.at[it, h, dx])
            for dy in (2, 1, 3, 0):
                gy = wrap(y + dy, NY)
                zs[it, h, core, gx, gy] += zc[it, h, gx, gy]
                if (dx, dy) != (0, 0):
                    send(
                        zs.at[it, h, core, gx, gy], rx.at[it, h, dx * NY + dy - 1],
                        rx_send.at[it, h], rx_recv.at[it, h], plane(dx, dy),
                    )

    def plane_sum(it, h):
        total = zs[it, h, core, x, y]
        arrived(rx.at[it, h], rx_recv.at[it, h])
        for k in range(NX * NY - 1):
            total += rx[it, h, k]
        return total

    for copy in vec_loads[:2]:
        copy.wait()
    pl.semaphore_wait(barrier, len(greeted))
    for h in range(2):
        gather_plane_start(0, h, 2.0 * vecs[NOW, half(h)] - vecs[PREV, half(h)])

    prod[SLOTS] = jnp.zeros((PARTS, 2, HALF, BATCH), F32)
    for copy in list_loads + vec_loads[2:]:
        copy.wait()
    live = live_ref[0, 0]
    keys = [
        jnp.where(s < live, rows_ref[0, s] * CB_DEV + cols_ref[0, s], -1) for s in range(SLOTS)
    ]
    for b in range(RB_DEV * CB_DEV):
        found = jnp.int32(SLOTS)
        for s in range(SLOTS):
            found = jnp.where(keys[s] == b, s, found)
        place[b] = found
    load.wait()

    def prepare(s, carry):
        value = blk[s]
        high, low = split(value)
        a_hi[s] = high
        a_lo[s] = low
        high, low = split(value.T)
        at_hi[s] = high
        at_lo[s] = low
        return carry

    lax.fori_loop(0, SLOTS, prepare, 0)

    for it in range(ITERS):
        for h in range(2):
            gather_plane_pass(it, h)
        for h in range(2):
            gather_plane_last(it, h)
        products(a_hi, a_lo, [cols_ref[0, s] for s in range(SLOTS)], xs)
        for h in range(2):
            ring_send(it, h)
        for h in range(2):
            ring_relay(it, h)
        for h in range(2):
            image = ring_sum(it, h)
            dual = jnp.maximum(vecs[DUAL, half(h)] + dual_step * (vecs[BOUND, half(h)] - image), 0.0)
            vecs[DUAL, half(h)] = dual
            gather_ring_start(it, h, dual)
        for h in range(2):
            gather_ring_relay(it, h)
        for h in range(2):
            gather_ring_finish(it, h)
        products(at_hi, at_lo, [rows_ref[0, s] for s in range(SLOTS)], ds)
        for h in range(2):
            plane_swap(it, h)
        for h in range(2):
            plane_send(it, h)
        for h in range(2):
            adjoint = plane_sum(it, h)
            before = vecs[NOW, half(h)]
            after = jnp.minimum(
                jnp.maximum(before - primal_step * (vecs[COST, half(h)] - adjoint), vecs[LOWER, half(h)]),
                vecs[UPPER, half(h)],
            )
            if it + 1 < ITERS:
                gather_plane_start(it + 1, h, 2.0 * after - before)
                vecs[NOW, half(h)] = after
            else:
                primal_out[half(h), :] = after
                dual_out[half(h), :] = vecs[DUAL, half(h)]
    for it in range(ITERS):
        for h in range(2):
            direct = rx.at[it, h]
            for sem in (xg_send, rz_send, dg_send, rx_send):
                waiter(direct, sem.at[it, h], sem.at[it, h]).wait_send()
            for sem in (xc_send, zc_send):
                waiter(zc.at[it, h], sem.at[it, h], sem.at[it, h]).wait_send()


def on_device(
    blocks, block_rows, block_cols, live_count, primal_now, primal_prev, dual_now, row_bound,
    objective, lower_bound, upper_bound,
):
    vmem = pl.BlockSpec(memory_space=pltpu.VMEM)
    dma = pltpu.SemaphoreType.DMA
    vec = jax.ShapeDtypeStruct((CHUNK, BATCH), F32)
    primal, dual = pl.pallas_call(
        kernel,
        out_shape=(vec, vec),
        in_specs=[pl.BlockSpec(memory_space=pl.ANY)] * 11,
        out_specs=(vmem, vmem),
        scratch_shapes=[
            pltpu.SMEM((1, SLOTS), jnp.int32),
            pltpu.SMEM((1, SLOTS), jnp.int32),
            pltpu.SMEM((1, 1), jnp.int32),
            pltpu.SMEM((RB_DEV * CB_DEV,), jnp.int32),
            pltpu.VMEM((7, CHUNK, BATCH), F32),
            pltpu.VMEM((SLOTS, BS, BS), F32),
            pltpu.VMEM((SLOTS, BS, BS), BF16),
            pltpu.VMEM((SLOTS, BS, BS), BF16),
            pltpu.VMEM((SLOTS, BS, BS), BF16),
            pltpu.VMEM((SLOTS, BS, BS), BF16),
            pltpu.VMEM((ITERS, 2, 2, NX, NY, HALF, BATCH), F32),
            pltpu.VMEM((2 * NX * NY, CHUNK, 2 * BATCH), BF16),
            pltpu.VMEM((SLOTS + 1, PARTS, 2, HALF, BATCH), F32),
            pltpu.VMEM((ITERS, 2, NZ, HALF, BATCH), F32),
            pltpu.VMEM((ITERS, 2, 2, 8, HALF, BATCH), F32),
            pltpu.VMEM((ITERS, 2, NZ, HALF, BATCH), F32),
            pltpu.VMEM((NZ, CHUNK, 2 * BATCH), BF16),
            pltpu.VMEM((ITERS, 2, 2, NX, NY, HALF, BATCH), F32),
            pltpu.VMEM((ITERS, 2, NX, NY, HALF, BATCH), F32),
            pltpu.VMEM((ITERS, 2, NX * NY - 1, HALF, BATCH), F32),
            dma, dma((3,)), dma((7,)),
            dma((ITERS, 2)), dma((ITERS, 2, NX)),
            dma((ITERS, 2)), dma((ITERS, 2, NX)),
            dma((ITERS, 2)), dma((ITERS, 2, 2, 3)),
            dma((ITERS, 2)), dma((ITERS, 2, NZ)),
            dma((ITERS, 2)), dma((ITERS, 2, NX)),
            dma((ITERS, 2)), dma((ITERS, 2)),
        ],
        compiler_params=pltpu.CompilerParams(
            collective_id=0, has_side_effects=True, vmem_limit_bytes=56 * 1024 * 1024
        ),
        name="pdhg",
    )(
        block_rows, block_cols, live_count, blocks[0],
        primal_now[0], primal_prev[0], dual_now[0], row_bound[0],
        objective[0], lower_bound[0], upper_bound[0],
    )
    return (primal[None], dual[None])


def solution(mesh):
    in_specs = (
        P("row", "col", None, None),
        P("row", "col"),
        P("row", "col"),
        P("row", "col"),
        P("col", "row", None),
        P("col", "row", None),
        P("row", "col", None),
        P("row", "col", None),
        P("col", "row", None),
        P("col", "row", None),
        P("col", "row", None),
    )
    out_specs = (P("col", "row", None), P("row", "col", None))
    return jax.shard_map(
        on_device, mesh=mesh, in_specs=in_specs, out_specs=out_specs, check_vma=False
    )
```

```python
import functools

import jax
import jax.numpy as jnp
from jax import lax
from jax.experimental import pallas as pl
from jax.experimental.pallas import tpu as pltpu
from jax.sharding import PartitionSpec as P

MESH = pl.DeviceIdType.MESH
F32 = jnp.float32
BF16 = jnp.bfloat16

NX, NY, NZ = 4, 4, 16
RB_DEV = 4
CB_DEV = 8
SLOTS = 12
BS = 256
ITERS = 2
BATCH = 128
CHUNK = 64
CUTS = 2
ROWS = CHUNK // CUTS
PARTS = BS // CHUNK

dual_step = 0.3
primal_step = 0.3

SIDES = (1, -1)
XY_PARTNERS = sorted(
    [(dx, dy) for dx in range(NX) for dy in range(NY) if (dx, dy) != (0, 0)],
    key=lambda d: -(min(d[0], NX - d[0]) + min(d[1], NY - d[1])),
)
FROM3, FROM4, FROM6, FROM7, FROM8, NEXT, SUM2, SUM5 = range(8)
FIRST_HOPS = ((FROM8, 8, 3), (FROM7, 7, 2), (FROM6, 6, 1), (FROM4, 4, -1), (FROM3, 3, 1), (NEXT, 1, 1))
SLOT_SUM = {FROM8: 0, FROM7: 0, FROM6: 0, FROM4: 0, FROM3: 1, NEXT: 2}
NOW, PREV, DUAL, BOUND, COST, LOWER, UPPER = range(7)


def split(value):
    high = value.astype(BF16)
    low = (value - high.astype(F32)).astype(BF16)
    return high, low


def kernel(
    rows_hbm, cols_hbm, live_hbm, blocks_hbm,
    now_hbm, prev_hbm, dual_hbm, bound_hbm, cost_hbm, lower_hbm, upper_hbm,
    result,
    rows_ref, cols_ref, live_ref, place,
    vecs, blk, a_hi, a_lo, at_hi, at_lo,
    xg, xs, prod, ys, rz, dg, ds, zs, zc, rx,
    blk_sem, list_sem, vec_sem,
    xg_send, xg_recv, xc_send, xc_recv,
    rz_send, rz_recv, dg_send, dg_recv,
    zc_send, zc_recv, rx_send, rx_recv,
):
    row = lax.axis_index("row")
    z = lax.axis_index("col")
    x = row // (2 * NY)
    y = (row // 2) % NY
    core = row % 2
    other = 1 - core

    def wrap(value, size):
        return lax.rem(value + size, size)

    def plane(dx, dy):
        return (wrap(x + dx, NX) * (2 * NY) + wrap(y + dy, NY) * 2 + core, z)

    def along(dz):
        return (row, wrap(z + dz, NZ))

    sibling = (row + 1 - 2 * core, z)

    barrier = pltpu.get_barrier_semaphore()
    greeted = [sibling] + [plane(dx, dy) for dx, dy in XY_PARTNERS]
    greeted += [along(sg * d) for d in (1, 2, 3, 5) for sg in SIDES]
    for device in greeted:
        pl.semaphore_signal(barrier, inc=1, device_id=device, device_id_type=MESH)

    vec_refs = (now_hbm, prev_hbm, dual_hbm, bound_hbm, cost_hbm, lower_hbm, upper_hbm)
    vec_loads = [pltpu.make_async_copy(ref, vecs.at[i], vec_sem.at[i]) for i, ref in enumerate(vec_refs)]
    list_loads = [
        pltpu.make_async_copy(src, dst, list_sem.at[i])
        for i, (src, dst) in enumerate(((rows_hbm, rows_ref), (cols_hbm, cols_ref), (live_hbm, live_ref)))
    ]
    load = pltpu.make_async_copy(blocks_hbm, blk, blk_sem)
    for copy in vec_loads[:2] + [load] + list_loads + vec_loads[2:]:
        copy.start()

    def send(src, dst, send_sem, recv_sem, device):
        copy = pltpu.make_async_remote_copy(
            src_ref=src, dst_ref=dst, send_sem=send_sem, recv_sem=recv_sem,
            device_id=device, device_id_type=MESH,
        )
        copy.start()
        return copy

    def waiter(ref, send_sem, recv_sem):
        return pltpu.make_async_remote_copy(
            src_ref=ref, dst_ref=ref, send_sem=send_sem, recv_sem=recv_sem,
            device_id=sibling, device_id_type=MESH,
        )

    def arrived(ref, recv_sem):
        waiter(ref, recv_sem, recv_sem).wait_recv()

    def rows_of(h):
        return pl.ds(h * ROWS, ROWS)

    def gather_plane_start(it, h, value):
        own = xg.at[it, h, core, x, y]
        own[...] = value
        for dx, dy in XY_PARTNERS:
            send(own, own, xg_send.at[it, h], xg_recv.at[it, h, dx], plane(dx, dy))

    def split_group(it, h, c, gx):
        for gy in range(NY):
            high, low = split(xg[it, h, c, gx, gy])
            at = gx * (2 * NY) + gy * 2 + c
            xs[at, rows_of(h), :BATCH] = high
            xs[at, rows_of(h), BATCH:] = low

    def gather_plane_pass(it, h):
        for dx in (0, 1, 3, 2):
            gx = wrap(x - dx, NX)
            group = xg.at[it, h, core, gx]
            arrived(group if dx else group.at[pl.ds(0, NY - 1)], xg_recv.at[it, h, dx])
            send(group, group, xc_send.at[it, h], xc_recv.at[it, h, dx], sibling)
            split_group(it, h, core, gx)

    def gather_plane_last(it, h):
        for dx in (0, 1, 3, 2):
            gx = wrap(x - dx, NX)
            arrived(xg.at[it, h, other, gx], xc_recv.at[it, h, dx])
            split_group(it, h, other, gx)

    def products(hi, lo, table, vec):
        for s in range(SLOTS):
            at = table[s]
            rhs = vec[pl.ds(at * PARTS, PARTS)].reshape(BS, 2 * BATCH)
            main = jnp.dot(hi[s], rhs, preferred_element_type=F32)
            rest = jnp.dot(lo[s], rhs[:, :BATCH], preferred_element_type=F32)
            prod[s] = (main[:, :BATCH] + main[:, BATCH:] + rest).reshape(PARTS, CUTS, ROWS, BATCH)

    def image_sums(it):
        for r in range(RB_DEV):
            total = prod[place[r * CB_DEV]]
            for c in range(1, CB_DEV):
                total += prod[place[r * CB_DEV + c]]
            ys[it, r * PARTS : (r + 1) * PARTS] = total

    def adjoint_sums(it):
        for cb in range(CB_DEV):
            total = prod[place[cb]]
            for r in range(1, RB_DEV):
                total += prod[place[r * CB_DEV + cb]]
            for part in range(PARTS):
                at = cb * PARTS + part
                gx, gy, c = at // (2 * NY), at // 2 % NY, at % 2
                for h in range(CUTS):
                    zs[it, h, c, gx, gy] = total[part, h]

    def side(sg):
        return (1 - sg) // 2

    def has(h, sg, slot):
        return slot != FROM8 or side(sg) == h % 2

    def ring_send(it, h):
        for slot, far, via in FIRST_HOPS:
            for sg in SIDES:
                if has(h, sg, slot):
                    zd = wrap(z + sg * far, NZ)
                    to = SLOT_SUM[slot]
                    send(
                        ys.at[it, zd, h], rz.at[it, h, side(sg), slot],
                        rz_send.at[it, h], rz_recv.at[it, h, side(sg), to], along(sg * via),
                    )

    def ring_relay(it, h):
        for to, far, parts in ((1, 2, (FROM3,)), (0, 5, (FROM4, FROM6, FROM7, FROM8))):
            for sg in SIDES:
                zd = wrap(z + sg * far, NZ)
                parts_here = [part for part in parts if has(h, sg, part)]
                first, count = parts_here[0], len(parts_here)
                arrived(rz.at[it, h, side(sg), pl.ds(first, count)], rz_recv.at[it, h, side(sg), to])
                total = ys[it, zd, h]
                for part in parts_here:
                    total += rz[it, h, side(sg), part]
                ys[it, zd, h] = total
                slot = SUM5 if far == 5 else SUM2
                send(
                    ys.at[it, zd, h], rz.at[it, h, side(sg), slot],
                    rz_send.at[it, h], rz_recv.at[it, h, side(sg), 2], along(sg * far),
                )

    def ring_sum(it, h):
        total = ys[it, z, h]
        for sg in SIDES:
            arrived(rz.at[it, h, side(sg), pl.ds(NEXT, 3)], rz_recv.at[it, h, side(sg), 2])
            for slot in (NEXT, SUM2, SUM5):
                total += rz[it, h, side(sg), slot]
        return total

    def ring_pass(it, h, far, via):
        ref = dg.at[it, h, wrap(z + via - far, NZ)]
        sem = far % NZ if abs(far) in (1, 2, 5) else 0
        send(ref, ref, dg_send.at[it, h], dg_recv.at[it, h, sem], along(via))

    def ring_split(it, h, far):
        at = wrap(z - far, NZ)
        high, low = split(dg[it, h, at])
        ds[at, rows_of(h), :BATCH] = high
        ds[at, rows_of(h), BATCH:] = low

    def ring_arrived(it, h, far):
        arrived(dg.at[it, h, 0], dg_recv.at[it, h, far % NZ])

    def gather_ring_start(it, h, value):
        dg[it, h, z] = value
        for far in (5, 2, 1):
            for sg in SIDES:
                ring_pass(it, h, sg * far, sg * far)
        ring_split(it, h, 0)

    def gather_ring_relay(it, h):
        for sg in SIDES:
            ring_arrived(it, h, 2 * sg)
            ring_pass(it, h, 3 * sg, sg)
        for sg in SIDES:
            ring_arrived(it, h, 5 * sg)
            if has(h, sg, FROM8):
                ring_pass(it, h, 8 * sg, 3 * sg)
            ring_pass(it, h, 7 * sg, 2 * sg)
            ring_pass(it, h, 6 * sg, sg)
            ring_pass(it, h, 4 * sg, -sg)
        for sg in SIDES:
            ring_arrived(it, h, sg)
            for far in (1, 2, 5):
                ring_split(it, h, far * sg)

    def gather_ring_finish(it, h):
        arrived(dg.at[it, h, pl.ds(0, 9)], dg_recv.at[it, h, 0])
        for far in (3, 4, 6, 7):
            for sg in SIDES:
                ring_split(it, h, sg * far)
        ring_split(it, h, 8)

    plane_order = (2, 1, 3, 0)

    def plane_swap(it, h):
        for dx in plane_order:
            gx = wrap(x + dx, NX)
            send(
                zs.at[it, h, other, gx], zc.at[it, h, gx],
                zc_send.at[it, h], zc_recv.at[it, h, dx], sibling,
            )

    def plane_send(it, h):
        for dx in plane_order:
            gx = wrap(x + dx, NX)
            arrived(zc.at[it, h, gx], zc_recv.at[it, h, dx])
            zs[it, h, core, gx] += zc[it, h, gx]
            for dy in (2, 1, 3, 0):
                if (dx, dy) != (0, 0):
                    send(
                        zs.at[it, h, core, gx, wrap(y + dy, NY)], rx.at[it, h, dx * NY + dy - 1],
                        rx_send.at[it, h], rx_recv.at[it, h], plane(dx, dy),
                    )

    def plane_sum(it, h):
        total = zs[it, h, core, x, y]
        arrived(rx.at[it, h], rx_recv.at[it, h])
        for k in range(NX * NY - 1):
            total += rx[it, h, k]
        return total

    for copy in vec_loads[:2]:
        copy.wait()
    pl.semaphore_wait(barrier, len(greeted))
    for h in range(CUTS):
        gather_plane_start(0, h, 2.0 * vecs[NOW, rows_of(h)] - vecs[PREV, rows_of(h)])

    prod[SLOTS] = jnp.zeros((PARTS, CUTS, ROWS, BATCH), F32)
    for copy in list_loads + vec_loads[2:]:
        copy.wait()
    live = live_ref[0, 0]
    keys = [
        jnp.where(s < live, rows_ref[0, s] * CB_DEV + cols_ref[0, s], -1) for s in range(SLOTS)
    ]
    for b in range(RB_DEV * CB_DEV):
        found = jnp.int32(SLOTS)
        for s in range(SLOTS):
            found = jnp.where(keys[s] == b, s, found)
        place[b] = found
    load.wait()

    def prepare(s, carry):
        value = blk[s]
        high, low = split(value)
        a_hi[s] = high
        a_lo[s] = low
        high, low = split(value.T)
        at_hi[s] = high
        at_lo[s] = low
        return carry

    lax.fori_loop(0, SLOTS, prepare, 0)

    for it in range(ITERS):
        for h in range(CUTS):
            gather_plane_pass(it, h)
        for h in range(CUTS):
            gather_plane_last(it, h)
        products(a_hi, a_lo, [cols_ref[0, s] for s in range(SLOTS)], xs)
        image_sums(it)
        for h in range(CUTS):
            ring_send(it, h)
        for h in range(CUTS):
            ring_relay(it, h)
        for h in range(CUTS):
            image = ring_sum(it, h)
            dual = jnp.maximum(vecs[DUAL, rows_of(h)] + dual_step * (vecs[BOUND, rows_of(h)] - image), 0.0)
            vecs[DUAL, rows_of(h)] = dual
            gather_ring_start(it, h, dual)
        for h in range(CUTS):
            gather_ring_relay(it, h)
        for h in range(CUTS):
            gather_ring_finish(it, h)
        products(at_hi, at_lo, [rows_ref[0, s] for s in range(SLOTS)], ds)
        adjoint_sums(it)
        for h in range(CUTS):
            plane_swap(it, h)
        for h in range(CUTS):
            plane_send(it, h)
        for h in range(CUTS):
            adjoint = plane_sum(it, h)
            before = vecs[NOW, rows_of(h)]
            after = jnp.minimum(
                jnp.maximum(before - primal_step * (vecs[COST, rows_of(h)] - adjoint), vecs[LOWER, rows_of(h)]),
                vecs[UPPER, rows_of(h)],
            )
            if it + 1 < ITERS:
                gather_plane_start(it + 1, h, 2.0 * after - before)
                vecs[NOW, rows_of(h)] = after
            else:
                result[0, rows_of(h), :] = after
                result[1, rows_of(h), :] = vecs[DUAL, rows_of(h)]
    for it in range(ITERS):
        for h in range(CUTS):
            direct = dg.at[it, h, pl.ds(0, NZ - 1)]
            for sem in (xg_send, rz_send, dg_send, rx_send):
                waiter(direct, sem.at[it, h], sem.at[it, h]).wait_send()
            for sem in (xc_send, zc_send):
                waiter(zc.at[it, h], sem.at[it, h], sem.at[it, h]).wait_send()


def on_device(
    blocks, block_rows, block_cols, live_count, primal_now, primal_prev, dual_now, row_bound,
    objective, lower_bound, upper_bound,
):
    vmem = pl.BlockSpec(memory_space=pltpu.VMEM)
    dma = pltpu.SemaphoreType.DMA
    result = pl.pallas_call(
        kernel,
        out_shape=jax.ShapeDtypeStruct((2, CHUNK, BATCH), F32),
        in_specs=[pl.BlockSpec(memory_space=pl.ANY)] * 11,
        out_specs=vmem,
        scratch_shapes=[
            pltpu.SMEM((1, SLOTS), jnp.int32),
            pltpu.SMEM((1, SLOTS), jnp.int32),
            pltpu.SMEM((1, 1), jnp.int32),
            pltpu.SMEM((RB_DEV * CB_DEV,), jnp.int32),
            pltpu.VMEM((7, CHUNK, BATCH), F32),
            pltpu.VMEM((SLOTS, BS, BS), F32),
            pltpu.VMEM((SLOTS, BS, BS), BF16),
            pltpu.VMEM((SLOTS, BS, BS), BF16),
            pltpu.VMEM((SLOTS, BS, BS), BF16),
            pltpu.VMEM((SLOTS, BS, BS), BF16),
            pltpu.VMEM((ITERS, CUTS, 2, NX, NY, ROWS, BATCH), F32),
            pltpu.VMEM((2 * NX * NY, CHUNK, 2 * BATCH), BF16),
            pltpu.VMEM((SLOTS + 1, PARTS, CUTS, ROWS, BATCH), F32),
            pltpu.VMEM((ITERS, NZ, CUTS, ROWS, BATCH), F32),
            pltpu.VMEM((ITERS, CUTS, 2, 8, ROWS, BATCH), F32),
            pltpu.VMEM((ITERS, CUTS, NZ, ROWS, BATCH), F32),
            pltpu.VMEM((NZ, CHUNK, 2 * BATCH), BF16),
            pltpu.VMEM((ITERS, CUTS, 2, NX, NY, ROWS, BATCH), F32),
            pltpu.VMEM((ITERS, CUTS, NX, NY, ROWS, BATCH), F32),
            pltpu.VMEM((ITERS, CUTS, NX * NY - 1, ROWS, BATCH), F32),
            dma, dma((3,)), dma((7,)),
            dma((ITERS, CUTS)), dma((ITERS, CUTS, NX)),
            dma((ITERS, CUTS)), dma((ITERS, CUTS, NX)),
            dma((ITERS, CUTS)), dma((ITERS, CUTS, 2, 3)),
            dma((ITERS, CUTS)), dma((ITERS, CUTS, NZ)),
            dma((ITERS, CUTS)), dma((ITERS, CUTS, NX)),
            dma((ITERS, CUTS)), dma((ITERS, CUTS)),
        ],
        compiler_params=pltpu.CompilerParams(
            collective_id=0, has_side_effects=True, vmem_limit_bytes=56 * 1024 * 1024
        ),
        name="pdhg",
    )(
        block_rows, block_cols, live_count, blocks[0],
        primal_now[0], primal_prev[0], dual_now[0], row_bound[0],
        objective[0], lower_bound[0], upper_bound[0],
    )
    return (result[:1], result[1:])


def solution(mesh):
    in_specs = (
        P("row", "col", None, None),
        P("row", "col"),
        P("row", "col"),
        P("row", "col"),
        P("col", "row", None),
        P("col", "row", None),
        P("row", "col", None),
        P("row", "col", None),
        P("col", "row", None),
        P("col", "row", None),
        P("col", "row", None),
    )
    out_specs = (P("col", "row", None), P("row", "col", None))
    return jax.shard_map(
        on_device, mesh=mesh, in_specs=in_specs, out_specs=out_specs, check_vma=False
    )
```

```python
import functools

import jax
import jax.numpy as jnp
from jax import lax
from jax.experimental import pallas as pl
from jax.experimental.pallas import tpu as pltpu
from jax.sharding import PartitionSpec as P

MESH = pl.DeviceIdType.MESH
F32 = jnp.float32
BF16 = jnp.bfloat16

NX, NY, NZ = 4, 4, 16
RB_DEV = 4
CB_DEV = 8
SLOTS = 12
BS = 256
ITERS = 2
BATCH = 128
CHUNK = 64
CUTS = 2
ROWS = CHUNK // CUTS
RING_CUTS = 4
RING_ROWS = CHUNK // RING_CUTS
PARTS = BS // CHUNK

dual_step = 0.3
primal_step = 0.3

SIDES = (1, -1)
XY_PARTNERS = sorted(
    [(dx, dy) for dx in range(NX) for dy in range(NY) if (dx, dy) != (0, 0)],
    key=lambda d: -(min(d[0], NX - d[0]) + min(d[1], NY - d[1])),
)
FROM3, FROM4, FROM6, FROM7, FROM8, NEXT, SUM2, SUM5 = range(8)
FIRST_HOPS = ((FROM8, 8, 3), (FROM7, 7, 2), (FROM6, 6, 1), (FROM4, 4, -1), (FROM3, 3, 1), (NEXT, 1, 1))
SLOT_SUM = {FROM8: 0, FROM7: 0, FROM6: 0, FROM4: 0, FROM3: 1, NEXT: 2}
NOW, PREV, DUAL, BOUND, COST, LOWER, UPPER = range(7)


def split(value):
    high = value.astype(BF16)
    low = (value - high.astype(F32)).astype(BF16)
    return high, low


def kernel(
    rows_hbm, cols_hbm, live_hbm, blocks_hbm,
    now_hbm, prev_hbm, dual_hbm, bound_hbm, cost_hbm, lower_hbm, upper_hbm,
    result,
    rows_ref, cols_ref, live_ref, place,
    vecs, blk, a_hi, a_lo, at_hi, at_lo,
    xg, xs, prod, ys, rz, dg, ds, zs, zc, rx,
    blk_sem, list_sem, vec_sem,
    xg_send, xg_recv, xc_send, xc_recv,
    rz_send, rz_recv, dg_send, dg_recv,
    zc_send, zc_recv, rx_send, rx_recv,
):
    row = lax.axis_index("row")
    z = lax.axis_index("col")
    x = row // (2 * NY)
    y = (row // 2) % NY
    core = row % 2
    other = 1 - core

    def wrap(value, size):
        return lax.rem(value + size, size)

    def plane(dx, dy):
        return (wrap(x + dx, NX) * (2 * NY) + wrap(y + dy, NY) * 2 + core, z)

    def along(dz):
        return (row, wrap(z + dz, NZ))

    sibling = (row + 1 - 2 * core, z)

    barrier = pltpu.get_barrier_semaphore()
    greeted = [sibling] + [plane(dx, dy) for dx, dy in XY_PARTNERS]
    greeted += [along(sg * d) for d in (1, 2, 3, 5) for sg in SIDES]
    for device in greeted:
        pl.semaphore_signal(barrier, inc=1, device_id=device, device_id_type=MESH)

    vec_refs = (now_hbm, prev_hbm, dual_hbm, bound_hbm, cost_hbm, lower_hbm, upper_hbm)
    vec_loads = [pltpu.make_async_copy(ref, vecs.at[i], vec_sem.at[i]) for i, ref in enumerate(vec_refs)]
    list_loads = [
        pltpu.make_async_copy(src, dst, list_sem.at[i])
        for i, (src, dst) in enumerate(((rows_hbm, rows_ref), (cols_hbm, cols_ref), (live_hbm, live_ref)))
    ]
    load = pltpu.make_async_copy(blocks_hbm, blk, blk_sem)
    for copy in vec_loads[:2] + [load] + list_loads + vec_loads[2:]:
        copy.start()

    def send(src, dst, send_sem, recv_sem, device):
        copy = pltpu.make_async_remote_copy(
            src_ref=src, dst_ref=dst, send_sem=send_sem, recv_sem=recv_sem,
            device_id=device, device_id_type=MESH,
        )
        copy.start()
        return copy

    def waiter(ref, send_sem, recv_sem):
        return pltpu.make_async_remote_copy(
            src_ref=ref, dst_ref=ref, send_sem=send_sem, recv_sem=recv_sem,
            device_id=sibling, device_id_type=MESH,
        )

    def arrived(ref, recv_sem):
        waiter(ref, recv_sem, recv_sem).wait_recv()

    def ring_rows(h):
        return pl.ds(h * RING_ROWS, RING_ROWS)

    def rows_of(h):
        return pl.ds(h * ROWS, ROWS)

    def gather_plane_start(it, h, value):
        own = xg.at[it, h, core, x, y]
        own[...] = value
        for dx, dy in XY_PARTNERS:
            send(own, own, xg_send.at[it, h], xg_recv.at[it, h, dx], plane(dx, dy))

    def split_group(it, h, c, gx):
        for gy in range(NY):
            high, low = split(xg[it, h, c, gx, gy])
            at = gx * (2 * NY) + gy * 2 + c
            xs[at, rows_of(h), :BATCH] = high
            xs[at, rows_of(h), BATCH:] = low

    def gather_plane_pass(it, h):
        for dx in (0, 1, 3, 2):
            gx = wrap(x - dx, NX)
            group = xg.at[it, h, core, gx]
            arrived(group if dx else group.at[pl.ds(0, NY - 1)], xg_recv.at[it, h, dx])
            send(group, group, xc_send.at[it, h], xc_recv.at[it, h, dx], sibling)
            split_group(it, h, core, gx)

    def gather_plane_last(it, h):
        for dx in (0, 1, 3, 2):
            gx = wrap(x - dx, NX)
            arrived(xg.at[it, h, other, gx], xc_recv.at[it, h, dx])
            split_group(it, h, other, gx)

    def products(hi, lo, table, vec):
        for s in range(SLOTS):
            at = table[s]
            rhs = vec[pl.ds(at * PARTS, PARTS)].reshape(BS, 2 * BATCH)
            main = jnp.dot(hi[s], rhs, preferred_element_type=F32)
            rest = jnp.dot(lo[s], rhs[:, :BATCH], preferred_element_type=F32)
            prod[s] = (main[:, :BATCH] + main[:, BATCH:] + rest).reshape(PARTS, CUTS, ROWS, BATCH)

    def image_sums(it):
        for r in range(RB_DEV):
            total = prod[place[r * CB_DEV]]
            for c in range(1, CB_DEV):
                total += prod[place[r * CB_DEV + c]]
            ys[it, r * PARTS : (r + 1) * PARTS] = total.reshape(PARTS, RING_CUTS, RING_ROWS, BATCH)

    def adjoint_sums(it):
        for cb in range(CB_DEV):
            total = prod[place[cb]]
            for r in range(1, RB_DEV):
                total += prod[place[r * CB_DEV + cb]]
            for part in range(PARTS):
                at = cb * PARTS + part
                gx, gy, c = at // (2 * NY), at // 2 % NY, at % 2
                for h in range(CUTS):
                    zs[it, h, c, gx, gy] = total[part, h]

    def side(sg):
        return (1 - sg) // 2

    def has(h, sg, slot):
        return slot != FROM8 or side(sg) == h % 2

    def ring_send(it, h):
        for slot, far, via in FIRST_HOPS:
            for sg in SIDES:
                if has(h, sg, slot):
                    zd = wrap(z + sg * far, NZ)
                    to = SLOT_SUM[slot]
                    send(
                        ys.at[it, zd, h], rz.at[it, h, side(sg), slot],
                        rz_send.at[it, h], rz_recv.at[it, h, side(sg), to], along(sg * via),
                    )

    def ring_relay(it, h):
        for to, far, parts in ((1, 2, (FROM3,)), (0, 5, (FROM4, FROM6, FROM7, FROM8))):
            for sg in SIDES:
                zd = wrap(z + sg * far, NZ)
                parts_here = [part for part in parts if has(h, sg, part)]
                first, count = parts_here[0], len(parts_here)
                arrived(rz.at[it, h, side(sg), pl.ds(first, count)], rz_recv.at[it, h, side(sg), to])
                total = ys[it, zd, h]
                for part in parts_here:
                    total += rz[it, h, side(sg), part]
                ys[it, zd, h] = total
                slot = SUM5 if far == 5 else SUM2
                send(
                    ys.at[it, zd, h], rz.at[it, h, side(sg), slot],
                    rz_send.at[it, h], rz_recv.at[it, h, side(sg), 2], along(sg * far),
                )

    def ring_sum(it, h):
        total = ys[it, z, h]
        for sg in SIDES:
            arrived(rz.at[it, h, side(sg), pl.ds(NEXT, 3)], rz_recv.at[it, h, side(sg), 2])
            for slot in (NEXT, SUM2, SUM5):
                total += rz[it, h, side(sg), slot]
        return total

    def ring_pass(it, h, far, via):
        ref = dg.at[it, h, wrap(z + via - far, NZ)]
        sem = far % NZ if abs(far) in (1, 2, 5) else 0
        send(ref, ref, dg_send.at[it, h], dg_recv.at[it, h, sem], along(via))

    def ring_split(it, h, far):
        at = wrap(z - far, NZ)
        high, low = split(dg[it, h, at])
        ds[at, ring_rows(h), :BATCH] = high
        ds[at, ring_rows(h), BATCH:] = low

    def ring_arrived(it, h, far):
        arrived(dg.at[it, h, 0], dg_recv.at[it, h, far % NZ])

    def gather_ring_start(it, h, value):
        dg[it, h, z] = value
        for far in (5, 2, 1):
            for sg in SIDES:
                ring_pass(it, h, sg * far, sg * far)
        ring_split(it, h, 0)

    def gather_ring_relay(it, h):
        for sg in SIDES:
            ring_arrived(it, h, 2 * sg)
            ring_pass(it, h, 3 * sg, sg)
        for sg in SIDES:
            ring_arrived(it, h, 5 * sg)
            if has(h, sg, FROM8):
                ring_pass(it, h, 8 * sg, 3 * sg)
            ring_pass(it, h, 7 * sg, 2 * sg)
            ring_pass(it, h, 6 * sg, sg)
            ring_pass(it, h, 4 * sg, -sg)
        for sg in SIDES:
            ring_arrived(it, h, sg)
            for far in (1, 2, 5):
                ring_split(it, h, far * sg)

    def gather_ring_finish(it, h):
        arrived(dg.at[it, h, pl.ds(0, 9)], dg_recv.at[it, h, 0])
        for far in (3, 4, 6, 7):
            for sg in SIDES:
                ring_split(it, h, sg * far)
        ring_split(it, h, 8)

    plane_order = (2, 1, 3, 0)

    def plane_swap(it, h):
        for dx in plane_order:
            gx = wrap(x + dx, NX)
            send(
                zs.at[it, h, other, gx], zc.at[it, h, gx],
                zc_send.at[it, h], zc_recv.at[it, h, dx], sibling,
            )

    def plane_send(it, h):
        for dx in plane_order:
            gx = wrap(x + dx, NX)
            arrived(zc.at[it, h, gx], zc_recv.at[it, h, dx])
            zs[it, h, core, gx] += zc[it, h, gx]
            for dy in (2, 1, 3, 0):
                if (dx, dy) != (0, 0):
                    send(
                        zs.at[it, h, core, gx, wrap(y + dy, NY)], rx.at[it, h, dx * NY + dy - 1],
                        rx_send.at[it, h], rx_recv.at[it, h], plane(dx, dy),
                    )

    def plane_sum(it, h):
        total = zs[it, h, core, x, y]
        arrived(rx.at[it, h], rx_recv.at[it, h])
        for k in range(NX * NY - 1):
            total += rx[it, h, k]
        return total

    for copy in vec_loads[:2]:
        copy.wait()
    pl.semaphore_wait(barrier, len(greeted))
    for h in range(CUTS):
        gather_plane_start(0, h, 2.0 * vecs[NOW, rows_of(h)] - vecs[PREV, rows_of(h)])

    prod[SLOTS] = jnp.zeros((PARTS, CUTS, ROWS, BATCH), F32)
    for copy in list_loads + vec_loads[2:]:
        copy.wait()
    live = live_ref[0, 0]
    keys = [
        jnp.where(s < live, rows_ref[0, s] * CB_DEV + cols_ref[0, s], -1) for s in range(SLOTS)
    ]
    for b in range(RB_DEV * CB_DEV):
        found = jnp.int32(SLOTS)
        for s in range(SLOTS):
            found = jnp.where(keys[s] == b, s, found)
        place[b] = found
    load.wait()

    def prepare(s, carry):
        value = blk[s]
        high, low = split(value)
        a_hi[s] = high
        a_lo[s] = low
        high, low = split(value.T)
        at_hi[s] = high
        at_lo[s] = low
        return carry

    lax.fori_loop(0, SLOTS, prepare, 0)

    for it in range(ITERS):
        for h in range(CUTS):
            gather_plane_pass(it, h)
        for h in range(CUTS):
            gather_plane_last(it, h)
        products(a_hi, a_lo, [cols_ref[0, s] for s in range(SLOTS)], xs)
        image_sums(it)
        for h in range(RING_CUTS):
            ring_send(it, h)
        for h in range(RING_CUTS):
            ring_relay(it, h)
        for h in range(RING_CUTS):
            image = ring_sum(it, h)
            dual = jnp.maximum(vecs[DUAL, ring_rows(h)] + dual_step * (vecs[BOUND, ring_rows(h)] - image), 0.0)
            vecs[DUAL, ring_rows(h)] = dual
            gather_ring_start(it, h, dual)
        for h in range(RING_CUTS):
            gather_ring_relay(it, h)
        for h in range(RING_CUTS):
            gather_ring_finish(it, h)
        products(at_hi, at_lo, [rows_ref[0, s] for s in range(SLOTS)], ds)
        adjoint_sums(it)
        for h in range(CUTS):
            plane_swap(it, h)
        for h in range(CUTS):
            plane_send(it, h)
        for h in range(CUTS):
            adjoint = plane_sum(it, h)
            before = vecs[NOW, rows_of(h)]
            after = jnp.minimum(
                jnp.maximum(before - primal_step * (vecs[COST, rows_of(h)] - adjoint), vecs[LOWER, rows_of(h)]),
                vecs[UPPER, rows_of(h)],
            )
            if it + 1 < ITERS:
                gather_plane_start(it + 1, h, 2.0 * after - before)
                vecs[NOW, rows_of(h)] = after
            else:
                result[0, rows_of(h), :] = after
                result[1, rows_of(h), :] = vecs[DUAL, rows_of(h)]
    for it in range(ITERS):
        for h in range(CUTS):
            for ref, sem in ((rx, xg_send), (rx, rx_send), (zc, xc_send), (zc, zc_send)):
                waiter(ref.at[it, h], sem.at[it, h], sem.at[it, h]).wait_send()
        for h in range(RING_CUTS):
            for sem in (rz_send, dg_send):
                waiter(dg.at[it, h, pl.ds(0, NZ - 1)], sem.at[it, h], sem.at[it, h]).wait_send()


def on_device(
    blocks, block_rows, block_cols, live_count, primal_now, primal_prev, dual_now, row_bound,
    objective, lower_bound, upper_bound,
):
    vmem = pl.BlockSpec(memory_space=pltpu.VMEM)
    dma = pltpu.SemaphoreType.DMA
    result = pl.pallas_call(
        kernel,
        out_shape=jax.ShapeDtypeStruct((2, CHUNK, BATCH), F32),
        in_specs=[pl.BlockSpec(memory_space=pl.ANY)] * 11,
        out_specs=vmem,
        scratch_shapes=[
            pltpu.SMEM((1, SLOTS), jnp.int32),
            pltpu.SMEM((1, SLOTS), jnp.int32),
            pltpu.SMEM((1, 1), jnp.int32),
            pltpu.SMEM((RB_DEV * CB_DEV,), jnp.int32),
            pltpu.VMEM((7, CHUNK, BATCH), F32),
            pltpu.VMEM((SLOTS, BS, BS), F32),
            pltpu.VMEM((SLOTS, BS, BS), BF16),
            pltpu.VMEM((SLOTS, BS, BS), BF16),
            pltpu.VMEM((SLOTS, BS, BS), BF16),
            pltpu.VMEM((SLOTS, BS, BS), BF16),
            pltpu.VMEM((ITERS, CUTS, 2, NX, NY, ROWS, BATCH), F32),
            pltpu.VMEM((2 * NX * NY, CHUNK, 2 * BATCH), BF16),
            pltpu.VMEM((SLOTS + 1, PARTS, CUTS, ROWS, BATCH), F32),
            pltpu.VMEM((ITERS, NZ, RING_CUTS, RING_ROWS, BATCH), F32),
            pltpu.VMEM((ITERS, RING_CUTS, 2, 8, RING_ROWS, BATCH), F32),
            pltpu.VMEM((ITERS, RING_CUTS, NZ, RING_ROWS, BATCH), F32),
            pltpu.VMEM((NZ, CHUNK, 2 * BATCH), BF16),
            pltpu.VMEM((ITERS, CUTS, 2, NX, NY, ROWS, BATCH), F32),
            pltpu.VMEM((ITERS, CUTS, NX, NY, ROWS, BATCH), F32),
            pltpu.VMEM((ITERS, CUTS, NX * NY - 1, ROWS, BATCH), F32),
            dma, dma((3,)), dma((7,)),
            dma((ITERS, CUTS)), dma((ITERS, CUTS, NX)),
            dma((ITERS, CUTS)), dma((ITERS, CUTS, NX)),
            dma((ITERS, RING_CUTS)), dma((ITERS, RING_CUTS, 2, 3)),
            dma((ITERS, RING_CUTS)), dma((ITERS, RING_CUTS, NZ)),
            dma((ITERS, CUTS)), dma((ITERS, CUTS, NX)),
            dma((ITERS, CUTS)), dma((ITERS, CUTS)),
        ],
        compiler_params=pltpu.CompilerParams(
            collective_id=0, has_side_effects=True, vmem_limit_bytes=56 * 1024 * 1024
        ),
        name="pdhg",
    )(
        block_rows, block_cols, live_count, blocks[0],
        primal_now[0], primal_prev[0], dual_now[0], row_bound[0],
        objective[0], lower_bound[0], upper_bound[0],
    )
    return (result[:1], result[1:])


def solution(mesh):
    in_specs = (
        P("row", "col", None, None),
        P("row", "col"),
        P("row", "col"),
        P("row", "col"),
        P("col", "row", None),
        P("col", "row", None),
        P("row", "col", None),
        P("row", "col", None),
        P("col", "row", None),
        P("col", "row", None),
        P("col", "row", None),
    )
    out_specs = (P("col", "row", None), P("row", "col", None))
    return jax.shard_map(
        on_device, mesh=mesh, in_specs=in_specs, out_specs=out_specs, check_vma=False
    )
```
